32 devices in a mesh: seq: 8 (over y, x, core), tp: 4 (over z).
Axes of the slice: x: 2, y: 2, z: 4, core: 2. Of those that a mesh axis runs over, the one named last changes fastest.
Arguments:
- frames: bfloat16 [640, 8, 1024], P('tp', 'seq'), may hold values from -6 to 6
- conv_weight: bfloat16 [9, 640, 640], P(None, 'tp'), may hold values from -0.078125 to 0.078125
- time_weight: bfloat16 [3, 640, 640], P(None, 'tp'), may hold values from -0.125 to 0.125
- cotangent: bfloat16 [640, 8, 1024], P('tp', 'seq'), may hold values from -6 to 6
Outputs:
- output: bfloat16 [640, 8, 1024], P('tp', 'seq')
- frame_grad: bfloat16 [640, 8, 1024], P('tp', 'seq')
- conv_grad: float32 [9, 640, 640], P(None, 'tp')
- time_grad: float32 [3, 640, 640], P(None, 'tp')
The draws below stay inside these ranges and needn't reach their ends.
All inputs are finite; a program needn't handle non-finite values.
Results may differ from the reference program's by a relative error of at most 0.0034.
Values may be sent and summed in bfloat16 or wider, within the bound.
A program may use at most 128 MiB of HBM per device.

```python
import jax
import jax.numpy as jnp
from jax import lax

C = 640
HGT = 32
WID = 32
FRAMES = 8
PLANE = 1024


def level_of(key, extent, pieces, low, largest):
    factor_of = 1.0
    for position, parts in pieces:
        draws = jax.random.uniform(jax.random.fold_in(jax.random.fold_in(key, 6), position), (parts,), jnp.float32, low / len(pieces), largest / len(pieces))
        factor_of = factor_of * jnp.repeat(jnp.exp(draws), extent[position] // parts).reshape((-1,) + (1,) * (len(extent) - 1 - position))
    return factor_of


def scatter_about(key, dims, deviation, most, cuts=(), dtype=jnp.bfloat16):
    entries = deviation * jax.random.normal(key, dims, jnp.float32)
    if cuts:
        entries = entries * level_of(key, dims, cuts, -0.22, 0.18)
    return jnp.clip(entries, -most, most).astype(dtype)


def setup_inputs(seed: int = 0) -> dict:
    streams_of = jax.random.split(jax.random.key(seed), 5)
    return {
        "frames": scatter_about(streams_of[0], (C, FRAMES, PLANE), 1.0, 6.0, ((0, 4), (1, 8))),
        "conv_weight": scatter_about(streams_of[1], (9, C, C), (9 * C) ** -0.5, 0.078125, ((1, 4),)),
        "time_weight": scatter_about(streams_of[2], (3, C, C), (3 * C) ** -0.5, 0.125, ((1, 4),)),
        "cotangent": scatter_about(streams_of[3], (C, FRAMES, PLANE), 1.0, 6.0, ((0, 4), (1, 8))),
    }


def shift_plane(field, down, right):
    leading = field.shape[:-1]
    plane = field.reshape(leading + (HGT, WID))
    padding = [(0, 0)] * len(leading) + [(1, 1), (1, 1)]
    padded = jnp.pad(plane, padding)
    moved = padded[..., 1 + down:1 + down + HGT, 1 + right:1 + right + WID]
    return moved.reshape(leading + (HGT * WID,))


def shift_frames(field, offset):
    padded = jnp.pad(field, ((0, 0), (1, 1), (0, 0)))
    return padded[:, 1 + offset:1 + offset + field.shape[1], :]


def flatten(field):
    return field.reshape(field.shape[0], -1)


def contract_first(weight, data):
    return lax.dot_general(weight, data, (((0,), (0,)), ((), ())), preferred_element_type=jnp.float32)


def contract_last(left_side, right_side):
    return lax.dot_general(left_side, right_side, (((1,), (1,)), ((), ())), preferred_element_type=jnp.float32)


def reference(frames, conv_weight, time_weight, cotangent):
    channels = frames.shape[0]
    frame_total = frames.shape[1]
    pre = jnp.zeros((channels, frame_total * HGT * WID), jnp.float32)
    for tap in range(9):
        moved = flatten(shift_plane(frames, tap // 3 - 1, tap % 3 - 1))
        pre = pre + jnp.dot(conv_weight[tap], moved, preferred_element_type=jnp.float32)
    pre = pre.reshape(frames.shape)
    act = jax.nn.silu(pre).astype(jnp.bfloat16)
    cot_flat = flatten(cotangent)
    mixed = jnp.zeros((channels, frame_total * HGT * WID), jnp.float32)
    time_parts = []
    for tap in range(3):
        window = flatten(shift_frames(act, tap - 1))
        mixed = mixed + jnp.dot(time_weight[tap], window, preferred_element_type=jnp.float32)
        time_parts.append(contract_last(cot_flat, window))
    output = (frames.astype(jnp.float32) + mixed.reshape(frames.shape)).astype(jnp.bfloat16)
    back = jnp.zeros((channels, frame_total * HGT * WID), jnp.float32)
    for tap in range(3):
        window = flatten(shift_frames(cotangent, 1 - tap))
        back = back + contract_first(time_weight[tap], window)
    sigmoid_pre = jax.nn.sigmoid(pre)
    slope = sigmoid_pre * (1.0 + pre * (1.0 - sigmoid_pre))
    pre_grad = (back.reshape(frames.shape) * slope).astype(jnp.bfloat16)
    pre_flat = flatten(pre_grad)
    frame_grad = cotangent.astype(jnp.float32)
    conv_parts = []
    for tap in range(9):
        down = tap // 3 - 1
        right = tap % 3 - 1
        spread = contract_first(conv_weight[tap], pre_flat)
        frame_grad = frame_grad + shift_plane(spread.reshape(frames.shape), -down, -right)
        moved = flatten(shift_plane(frames, down, right))
        conv_parts.append(contract_last(pre_flat, moved))
    conv_grad = jnp.stack(conv_parts) / frame_total
    time_grad = jnp.stack(time_parts) / frame_total
    return (output, frame_grad.astype(jnp.bfloat16), conv_grad, time_grad)
```

```python
import functools

import jax
import jax.numpy as jnp
from jax import lax
from jax.experimental import pallas as pl
from jax.experimental.pallas import tpu as pltpu
from jax.sharding import PartitionSpec as P

HGT = 32
WID = 32
BF = jnp.bfloat16
F32 = jnp.float32


def moved(x, down, right):
    if down == 0 and right == 0:
        return x
    plane = x.shape[-1]
    step = (-(WID * down + right)) % plane
    out = pltpu.roll(x, step, 1)
    where = lax.broadcasted_iota(jnp.int32, (1, plane), 1)
    row = where // WID + down
    col = where % WID + right
    ok = (row >= 0) & (row < HGT) & (col >= 0) & (col < WID)
    return jnp.where(ok, out, 0.0)


def nt(a, b):
    return lax.dot_general(a, b, (((1,), (1,)), ((), ())), preferred_element_type=F32)


def tn(a, b):
    return lax.dot_general(a, b, (((0,), (0,)), ((), ())), preferred_element_type=F32)


def nn(a, b):
    return jnp.dot(a, b, preferred_element_type=F32)


def kernel(
    ns, nz, q,
    fr, cw, tw, twt, cot,
    out, fgrad, cgrad, tgrad,
    ffull, cfull, afull, twr, chalo, prod, pre, qself, qsend, qrecv, ysend, yrecv,
    shifted, g, gsib, halfb, xin, full, fgsend, fgrecv,
    s_f, r_f, s_c, r_c, s_t, r_t, s_a, r_a, s_g, r_g,
    s_h, r_h, s_q, r_q, s_y, r_y, s_core, r_core, s_x, r_x, s_ag, r_ag, s_fw, r_fw,
):
    me = lax.axis_index("seq")
    z = lax.axis_index("tp")
    core = lax.rem(me, 2)
    chip = me // 2
    nc = ns // 2
    hr = nc * q
    loc = fr.shape[0]
    chans = nz * loc

    def zpeer(d):
        return {"tp": lax.rem(z + d, nz)}

    def speer(d):
        return {"seq": lax.rem(me + d + ns, ns)}

    def cpeer(d):
        return {"seq": lax.rem(chip + d, nc) * 2 + core}

    sib = {"seq": chip * 2 + (1 - core)}

    def remote(src, dst, ssem, rsem, dev):
        return pltpu.make_async_remote_copy(
            src_ref=src, dst_ref=dst, send_sem=ssem, recv_sem=rsem,
            device_id=dev, device_id_type=pl.DeviceIdType.MESH,
        )

    barrier = pltpu.get_barrier_semaphore()
    for d in range(1, nz):
        pl.semaphore_signal(barrier, inc=1, device_id=zpeer(d), device_id_type=pl.DeviceIdType.MESH)
    for d in range(1, ns):
        pl.semaphore_signal(barrier, inc=1, device_id=speer(d), device_id_type=pl.DeviceIdType.MESH)
    pl.semaphore_wait(barrier, nz - 1 + ns - 1)

    everything = []

    def go(copies):
        for c in copies:
            c.start()
        everything.extend(copies)
        return copies

    def arrived(copies):
        for c in copies:
            c.wait_recv()

    order = [1, nz - 1] + list(range(2, nz - 1))
    cf = go([remote(fr, ffull.at[z], s_f.at[d], r_f.at[d], zpeer(d)) for d in order])
    cc = go([remote(cot, cfull.at[z], s_c.at[d], r_c.at[d], zpeer(d)) for d in order])
    ct = go([
        remote(twt.at[lax.rem(z + d, nz)], twr.at[z], s_t.at[d], r_t.at[d], zpeer(d))
        for d in order
    ])
    ch = go([
        remote(cot, chalo.at[0], s_h.at[0], r_h.at[0], speer(1)),
        remote(cot, chalo.at[1], s_h.at[1], r_h.at[1], speer(-1)),
    ])
    ffull[z] = fr[...]
    cfull[z] = cot[...]
    twr[z] = twt[z]
    if 2 * hr > 3 * loc:
        for k in range(4):
            g[k, pl.ds(3 * loc, 2 * hr - 3 * loc), :] = jnp.zeros(
                (2 * hr - 3 * loc, chans), F32
            )
    arrived(cf)

    @pl.loop(0, 9)
    def _(t):
        prod[t] = nn(cw[t], ffull[...].reshape(chans, -1))

    total = prod[4]
    for t in range(9):
        if t != 4:
            total = total + moved(prod[t], t // 3 - 1, t % 3 - 1)
    pre[...] = total
    afull[z] = (total / (1.0 + jnp.exp(-total))).astype(BF)
    ca = go([remote(afull.at[z], afull.at[z], s_a.at[d], r_a.at[d], zpeer(d)) for d in order])

    arrived(cc)
    arrived(ct)

    def back_of(k):
        acc = nn(twr[0, k], cfull[0])
        for i in range(1, nz):
            acc = acc + nn(twr[i, k], cfull[i])
        return acc

    qsend[0] = back_of(0)
    qsend[1] = back_of(2)
    cq = go([
        remote(qsend.at[0], qrecv.at[0], s_q.at[0], r_q.at[0], speer(-1)),
        remote(qsend.at[1], qrecv.at[1], s_q.at[1], r_q.at[1], speer(1)),
    ])
    qself[...] = back_of(1)
    arrived(cq)
    back = qself[...]
    back = back + jnp.where(me < ns - 1, qrecv[0], 0.0)
    back = back + jnp.where(me > 0, qrecv[1], 0.0)
    pr = pre[...]
    sg = 1.0 / (1.0 + jnp.exp(-pr))
    pg = (back * sg * (1.0 + pr * (1.0 - sg))).astype(BF).astype(F32)
    for t in range(9):
        shifted[t] = moved(pg, 1 - t // 3, 1 - t % 3).astype(BF)

    other = pl.ds(pl.multiple_of((1 - core) * hr, 16), hr)
    mine = pl.ds(pl.multiple_of(core * hr, 16), hr)

    def core_send(k):
        return go([
            remote(g.at[k, other], gsib.at[k], s_core.at[k], r_core.at[k], sib)
        ])

    def chip_send(k):
        gsib[k] = g[k, mine, :] + gsib[k]
        halfb[k] = gsib[k].astype(BF)
        return go([
            remote(
                halfb.at[k, pl.ds(pl.multiple_of(lax.rem(chip + d, nc) * q, 16), q)],
                xin.at[k, d - 1], s_x.at[k, d - 1], r_x.at[k, d - 1], cpeer(d),
            )
            for d in range(1, nc)
        ])

    def chip_sum(k):
        acc = gsib[k, pl.ds(pl.multiple_of(chip * q, 16), q), :]
        for d in range(1, nc):
            acc = acc + xin[k, d - 1].astype(F32)
        own = pl.ds(pl.multiple_of(core * hr + chip * q, 16), q)
        full[k, own, :] = acc.astype(BF)
        return go([
            remote(
                full.at[k, own], full.at[k, own],
                s_ag.at[k, d - 1], r_ag.at[k, d - 1], cpeer(d),
            )
            for d in range(1, nc)
        ])

    def forward(k):
        return go([
            remote(full.at[k, mine], full.at[k, mine], s_fw.at[k], r_fw.at[k], sib)
        ])

    ccore, cx, cag, cfw = {}, {}, {}, {}
    for u in range(3):
        @pl.loop(0, 3)
        def _(v):
            g[u, pl.ds(pl.multiple_of(v * loc, 16), loc), :] = nt(
                shifted[3 * u + v], ffull[...].reshape(chans, -1)
            )
        ccore[u] = core_send(u)
        if u > 0:
            arrived(ccore[u - 1])
            cx[u - 1] = chip_send(u - 1)

    arrived(ca)
    arrived(ch)

    def time_part(k, rows):
        g[3, pl.ds(k * loc, loc), :] = nt(rows, afull[...].reshape(chans, -1))

    time_part(0, jnp.where(me < ns - 1, chalo[1], jnp.zeros_like(chalo[1])))
    time_part(1, cot[...])
    time_part(2, jnp.where(me > 0, chalo[0], jnp.zeros_like(chalo[0])))
    ccore[3] = core_send(3)
    arrived(ccore[2])
    cx[2] = chip_send(2)

    ysend[0] = nn(tw[0], afull[...].reshape(chans, -1)).astype(BF)
    ysend[1] = nn(tw[2], afull[...].reshape(chans, -1)).astype(BF)
    cy = go([
        remote(ysend.at[0], yrecv.at[0], s_y.at[0], r_y.at[0], speer(1)),
        remote(ysend.at[1], yrecv.at[1], s_y.at[1], r_y.at[1], speer(-1)),
    ])
    arrived(ccore[3])
    cx[3] = chip_send(3)

    prod[0:nz] = tn(cw[0], shifted[0]).reshape(nz, loc, -1)

    @pl.loop(1, 9)
    def _(t):
        prod[0:nz] += tn(cw[t], shifted[t]).reshape(nz, loc, -1)

    for i in range(nz):
        fgsend[i] = prod[i].astype(BF)
    cg = go([
        remote(fgsend.at[lax.rem(z + d, nz)], fgrecv.at[d - 1], s_g.at[d], r_g.at[d], zpeer(d))
        for d in order
    ])
    for k in range(4):
        arrived(cx[k])
        cag[k] = chip_sum(k)

    mix = nn(tw[1], afull[...].reshape(chans, -1))
    arrived(cy)
    mix = mix + jnp.where(me > 0, yrecv[0].astype(F32), 0.0)
    mix = mix + jnp.where(me < ns - 1, yrecv[1].astype(F32), 0.0)
    out[...] = (fr[...].astype(F32) + mix).astype(BF)

    for k in range(4):
        arrived(cag[k])
        cfw[k] = forward(k)

    arrived(cg)
    acc = cot[...].astype(F32) + prod[z]
    for d in range(nz - 1):
        acc = acc + fgrecv[d].astype(F32)
    fgrad[...] = acc.astype(BF)

    for k in range(4):
        arrived(cfw[k])
        for v in range(3):
            piece = full[k, v * loc:(v + 1) * loc, :].astype(F32) / ns
            if k < 3:
                cgrad[3 * k + v] = piece
            else:
                tgrad[v] = piece
    for c in everything:
        c.wait_send()


def per_device(frames, conv_weight, time_weight, cotangent):
    loc, count, plane = frames.shape
    ns, nz = lax.axis_size("seq"), lax.axis_size("tp")
    chans = conv_weight.shape[2]
    q = 16 * (-(-3 * loc // (16 * ns)))
    nc = ns // 2
    hr = nc * q
    twt = jnp.transpose(time_weight.reshape(3, loc, nz, loc), (2, 0, 3, 1))
    dma = pltpu.SemaphoreType.DMA
    V = pltpu.VMEM
    sems = [dma((nz,))] * 10 + [dma((2,))] * 6 + [dma((4,))] * 2
    sems += [dma((4, nc - 1))] * 4 + [dma((4,))] * 2
    outs = pl.pallas_call(
        functools.partial(kernel, ns, nz, q),
        out_shape=(
            jax.ShapeDtypeStruct((loc, plane), BF),
            jax.ShapeDtypeStruct((loc, plane), BF),
            jax.ShapeDtypeStruct((9, loc, chans), F32),
            jax.ShapeDtypeStruct((3, loc, chans), F32),
        ),
        in_specs=[pl.BlockSpec(memory_space=pltpu.VMEM)] * 5,
        out_specs=(pl.BlockSpec(memory_space=pltpu.VMEM),) * 4,
        scratch_shapes=[
            V((nz, loc, plane), BF),
            V((nz, loc, plane), BF),
            V((nz, loc, plane), BF),
            V((nz, 3, loc, loc), BF),
            V((2, loc, plane), BF),
            V((9, loc, plane), F32),
            V((loc, plane), F32),
            V((loc, plane), F32),
            V((2, loc, plane), F32),
            V((2, loc, plane), F32),
            V((2, loc, plane), BF),
            V((2, loc, plane), BF),
            V((9, loc, plane), BF),
            V((4, 2 * hr, chans), F32),
            V((4, hr, chans), F32),
            V((4, hr, chans), BF),
            V((4, nc - 1, q, chans), BF),
            V((4, 2 * hr, chans), BF),
            V((nz, loc, plane), BF),
            V((nz - 1, loc, plane), BF),
        ] + sems,
        compiler_params=pltpu.CompilerParams(
            collective_id=0, has_side_effects=True, vmem_limit_bytes=58 * 1024 * 1024
        ),
    )(
        frames.reshape(loc, plane), conv_weight, time_weight, twt,
        cotangent.reshape(loc, plane),
    )
    return (
        outs[0].reshape(frames.shape), outs[1].reshape(frames.shape), outs[2], outs[3],
    )


def solution(mesh):
    placed = (P("tp", "seq", None), P(None, "tp", None), P(None, "tp", None), P("tp", "seq", None))
    return jax.shard_map(
        per_device,
        mesh=mesh,
        in_specs=placed,
        out_specs=(
            P("tp", "seq", None),
            P("tp", "seq", None),
            P(None, "tp", None),
            P(None, "tp", None),
        ),
        check_vma=False,
    )
```

```python
import functools

import jax
import jax.numpy as jnp
from jax import lax
from jax.experimental import pallas as pl
from jax.experimental.pallas import tpu as pltpu
from jax.sharding import PartitionSpec as P

HGT = 32
WID = 32
BF = jnp.bfloat16
F32 = jnp.float32


def moved(x, down, right):
    if down == 0 and right == 0:
        return x
    plane = x.shape[-1]
    step = (-(WID * down + right)) % plane
    out = pltpu.roll(x, step, 1)
    where = lax.broadcasted_iota(jnp.int32, (1, plane), 1)
    row = where // WID + down
    col = where % WID + right
    ok = (row >= 0) & (row < HGT) & (col >= 0) & (col < WID)
    return jnp.where(ok, out, 0.0)


def nt(a, b):
    return lax.dot_general(a, b, (((1,), (1,)), ((), ())), preferred_element_type=F32)


def tn(a, b):
    return lax.dot_general(a, b, (((0,), (0,)), ((), ())), preferred_element_type=F32)


def nn(a, b):
    return jnp.dot(a, b, preferred_element_type=F32)


def kernel(
    ns, nz, q,
    fr, cw, tw, twt, cot,
    out, fgrad, cgrad, tgrad,
    ffull, cfull, afull, twr, chalo, prod, pre, qrecv, ysend, yrecv,
    shifted, g, gsib, halfb, xin, full, fgsend, fgrecv,
    s_f, r_f, s_c, r_c, s_t, r_t, s_a, r_a, s_g, r_g,
    s_h, r_h, s_q, r_q, s_y, r_y, s_core, r_core, s_x, r_x, s_ag, r_ag, s_fw, r_fw, s_u, r_u,
):
    me = lax.axis_index("seq")
    z = lax.axis_index("tp")
    core = lax.rem(me, 2)
    chip = me // 2
    nc = ns // 2
    hr = nc * q
    loc = fr.shape[0]
    chans = nz * loc

    def zpeer(d):
        return {"tp": lax.rem(z + d, nz)}

    def speer(d):
        return {"seq": lax.rem(me + d + ns, ns)}

    def cpeer(d):
        return {"seq": lax.rem(chip + d, nc) * 2 + core}

    sib = {"seq": chip * 2 + (1 - core)}

    def remote(src, dst, ssem, rsem, dev):
        return pltpu.make_async_remote_copy(
            src_ref=src, dst_ref=dst, send_sem=ssem, recv_sem=rsem,
            device_id=dev, device_id_type=pl.DeviceIdType.MESH,
        )

    barrier = pltpu.get_barrier_semaphore()
    for d in range(1, nz):
        pl.semaphore_signal(barrier, inc=1, device_id=zpeer(d), device_id_type=pl.DeviceIdType.MESH)
    for d in range(1, ns):
        pl.semaphore_signal(barrier, inc=1, device_id=speer(d), device_id_type=pl.DeviceIdType.MESH)
    pl.semaphore_wait(barrier, nz - 1 + ns - 1)

    everything = []

    def go(copies):
        for c in copies:
            c.start()
        everything.extend(copies)
        return copies

    def arrived(copies):
        for c in copies:
            c.wait_recv()

    order = [1, nz - 1] + list(range(2, nz - 1))
    lh = loc // 2
    hops = nz - 1

    def line_copy(buf, ssem, rsem, way, h):
        shard = z - h if way == 0 else z + h
        return remote(
            buf.at[shard], buf.at[shard], ssem.at[way, h], rsem.at[way, h],
            {"tp": z + 1 if way == 0 else z - 1},
        )

    def can_send(way, h):
        if way == 0:
            return (z - h >= 0) & (z + 1 < nz)
        return (z + h < nz) & (z - 1 >= 0)

    def line_send(line, h):
        for way in range(2):
            @pl.when(can_send(way, h))
            def _():
                line_copy(*line, way, h).start()

    def line_recv(line, h):
        buf, ssem, rsem = line
        for way in range(2):
            shard = z - 1 - h if way == 0 else z + 1 + h

            @pl.when(shard >= 0 if way == 0 else shard < nz)
            def _():
                remote(
                    buf.at[shard], buf.at[shard], ssem.at[way, h], rsem.at[way, h],
                    {"tp": z - 1 if way == 0 else z + 1},
                ).wait_recv()

    def line_step(line, h):
        line_recv(line, h)
        if h + 1 < hops:
            line_send(line, h + 1)

    def line_end(line):
        for h in range(hops):
            for way in range(2):
                @pl.when(can_send(way, h))
                def _():
                    line_copy(*line, way, h).wait_send()

    lf, lc, la = (ffull, s_f, r_f), (cfull, s_c, r_c), (afull, s_a, r_a)
    ffull[z] = fr[...]
    line_send(lf, 0)
    cfull[z] = cot[...]
    ch = go([
        remote(cot, chalo.at[0], s_h.at[0], r_h.at[0], speer(1)),
        remote(cot, chalo.at[1], s_h.at[1], r_h.at[1], speer(-1)),
    ])
    rows = pl.ds(pl.multiple_of(core * lh, 16), lh)
    ct = go([
        remote(
            twt.at[lax.rem(z + d, nz), :, rows], twr.at[z, :, rows],
            s_t.at[d], r_t.at[d], zpeer(d),
        )
        for d in order
    ])
    twr[z] = twt[z]
    if 2 * hr > 3 * loc:
        for k in range(4):
            g[k, pl.ds(3 * loc, 2 * hr - 3 * loc), :] = jnp.zeros(
                (2 * hr - 3 * loc, chans), F32
            )
    line_step(lf, 0)
    line_send(lc, 0)
    for h in range(1, hops):
        line_step(lf, h)
        line_step(lc, h - 1)
    cu = []
    for k, d in enumerate(order):
        ct[k].wait_recv()
        part = twr.at[lax.rem(z + nz - d, nz), :, rows]
        cu += go([remote(part, part, s_u.at[d], r_u.at[d], sib)])

    @pl.loop(0, 9)
    def _(t):
        prod[t] = nn(cw[t], ffull[...].reshape(chans, -1))

    total = prod[4]
    for t in range(9):
        if t != 4:
            total = total + moved(prod[t], t // 3 - 1, t % 3 - 1)
    pre[...] = total
    afull[z] = (total / (1.0 + jnp.exp(-total))).astype(BF)
    line_send(la, 0)
    line_step(lc, hops - 1)
    arrived(cu)

    def back_of(k):
        acc = nn(twr[0, k], cfull[0])
        for i in range(1, nz):
            acc = acc + nn(twr[i, k], cfull[i])
        return acc

    prod[5] = back_of(0)
    prod[6] = back_of(2)
    cq = go([
        remote(prod.at[5], qrecv.at[0], s_q.at[0], r_q.at[0], speer(-1)),
        remote(prod.at[6], qrecv.at[1], s_q.at[1], r_q.at[1], speer(1)),
    ])
    prod[8] = back_of(1)
    line_step(la, 0)
    arrived(cq)
    back = prod[8]
    back = back + jnp.where(me < ns - 1, qrecv[0], 0.0)
    back = back + jnp.where(me > 0, qrecv[1], 0.0)
    pr = pre[...]
    sg = 1.0 / (1.0 + jnp.exp(-pr))
    pg = (back * sg * (1.0 + pr * (1.0 - sg))).astype(BF).astype(F32)
    for t in range(9):
        shifted[t] = moved(pg, 1 - t // 3, 1 - t % 3).astype(BF)

    if hops > 1:
        line_step(la, 1)
    prod[0:nz] = tn(cw[0], shifted[0]).reshape(nz, loc, -1)

    @pl.loop(1, 9)
    def _(t):
        prod[0:nz] += tn(cw[t], shifted[t]).reshape(nz, loc, -1)

    for i in range(nz):
        fgsend[i] = prod[i].astype(BF)
    cg = go([
        remote(fgsend.at[lax.rem(z + d, nz)], fgrecv.at[d - 1], s_g.at[d], r_g.at[d], zpeer(d))
        for d in order
    ])

    other = pl.ds(pl.multiple_of((1 - core) * hr, 16), hr)
    mine = pl.ds(pl.multiple_of(core * hr, 16), hr)

    def core_send(k):
        return go([
            remote(g.at[k, other], gsib.at[k], s_core.at[k], r_core.at[k], sib)
        ])

    def chip_send(k):
        gsib[k] = g[k, mine, :] + gsib[k]
        halfb[k] = gsib[k].astype(BF)
        return go([
            remote(
                halfb.at[k, pl.ds(pl.multiple_of(lax.rem(chip + d, nc) * q, 16), q)],
                xin.at[k, d - 1], s_x.at[k, d - 1], r_x.at[k, d - 1], cpeer(d),
            )
            for d in range(1, nc)
        ])

    def chip_sum(k):
        acc = gsib[k, pl.ds(pl.multiple_of(chip * q, 16), q), :]
        for d in range(1, nc):
            acc = acc + xin[k, d - 1].astype(F32)
        own = pl.ds(pl.multiple_of(core * hr + chip * q, 16), q)
        full[k, own, :] = acc.astype(BF)
        return go([
            remote(
                full.at[k, own], full.at[k, own],
                s_ag.at[k, d - 1], r_ag.at[k, d - 1], cpeer(d),
            )
            for d in range(1, nc)
        ])

    def forward(k):
        return go([
            remote(full.at[k, mine], full.at[k, mine], s_fw.at[k], r_fw.at[k], sib)
        ])

    ccore, cx, cag, cfw = {}, {}, {}, {}
    for u in range(3):
        @pl.loop(0, 3)
        def _(v):
            g[u, pl.ds(pl.multiple_of(v * loc, 16), loc), :] = nt(
                shifted[3 * u + v], ffull[...].reshape(chans, -1)
            )
        ccore[u] = core_send(u)
        if u > 0:
            arrived(ccore[u - 1])
            cx[u - 1] = chip_send(u - 1)

    for h in range(2, hops):
        line_step(la, h)
    arrived(ch)

    def time_part(k, rows):
        g[3, pl.ds(k * loc, loc), :] = nt(rows, afull[...].reshape(chans, -1))

    time_part(0, jnp.where(me < ns - 1, chalo[1], jnp.zeros_like(chalo[1])))
    time_part(1, cot[...])
    time_part(2, jnp.where(me > 0, chalo[0], jnp.zeros_like(chalo[0])))
    ccore[3] = core_send(3)
    arrived(ccore[2])
    cx[2] = chip_send(2)

    ysend[0] = nn(tw[0], afull[...].reshape(chans, -1)).astype(BF)
    ysend[1] = nn(tw[2], afull[...].reshape(chans, -1)).astype(BF)
    cy = go([
        remote(ysend.at[0], yrecv.at[0], s_y.at[0], r_y.at[0], speer(1)),
        remote(ysend.at[1], yrecv.at[1], s_y.at[1], r_y.at[1], speer(-1)),
    ])
    arrived(ccore[3])
    cx[3] = chip_send(3)

    for k in range(4):
        arrived(cx[k])
        cag[k] = chip_sum(k)

    mix = nn(tw[1], afull[...].reshape(chans, -1))
    arrived(cy)
    mix = mix + jnp.where(me > 0, yrecv[0].astype(F32), 0.0)
    mix = mix + jnp.where(me < ns - 1, yrecv[1].astype(F32), 0.0)
    out[...] = (fr[...].astype(F32) + mix).astype(BF)

    for k in range(4):
        arrived(cag[k])
        cfw[k] = forward(k)

    arrived(cg)
    acc = cot[...].astype(F32) + prod[z]
    for d in range(nz - 1):
        acc = acc + fgrecv[d].astype(F32)
    fgrad[...] = acc.astype(BF)

    for k in range(4):
        arrived(cfw[k])
        for v in range(3):
            piece = full[k, v * loc:(v + 1) * loc, :].astype(F32) / ns
            if k < 3:
                cgrad[3 * k + v] = piece
            else:
                tgrad[v] = piece
    for c in everything:
        c.wait_send()
    for line in (lf, lc, la):
        line_end(line)


def per_device(frames, conv_weight, time_weight, cotangent):
    loc, count, plane = frames.shape
    ns, nz = lax.axis_size("seq"), lax.axis_size("tp")
    chans = conv_weight.shape[2]
    q = 16 * (-(-3 * loc // (16 * ns)))
    nc = ns // 2
    hr = nc * q
    twt = jnp.transpose(time_weight.reshape(3, loc, nz, loc), (2, 0, 3, 1))
    dma = pltpu.SemaphoreType.DMA
    V = pltpu.VMEM
    sems = [dma((2, nz))] * 4 + [dma((nz,))] * 2 + [dma((2, nz))] * 2 + [dma((nz,))] * 2 + [dma((2,))] * 6 + [dma((4,))] * 2
    sems += [dma((4, nc - 1))] * 4 + [dma((4,))] * 2 + [dma((nz,))] * 2
    outs = pl.pallas_call(
        functools.partial(kernel, ns, nz, q),
        out_shape=(
            jax.ShapeDtypeStruct((loc, plane), BF),
            jax.ShapeDtypeStruct((loc, plane), BF),
            jax.ShapeDtypeStruct((9, loc, chans), F32),
            jax.ShapeDtypeStruct((3, loc, chans), F32),
        ),
        in_specs=[pl.BlockSpec(memory_space=pltpu.VMEM)] * 5,
        out_specs=(pl.BlockSpec(memory_space=pltpu.VMEM),) * 4,
        scratch_shapes=[
            V((nz, loc, plane), BF),
            V((nz, loc, plane), BF),
            V((nz, loc, plane), BF),
            V((nz, 3, loc, loc), BF),
            V((2, loc, plane), BF),
            V((9, loc, plane), F32),
            V((loc, plane), F32),
            V((2, loc, plane), F32),
            V((2, loc, plane), BF),
            V((2, loc, plane), BF),
            V((9, loc, plane), BF),
            V((4, 2 * hr, chans), F32),
            V((4, hr, chans), F32),
            V((4, hr, chans), BF),
            V((4, nc - 1, q, chans), BF),
            V((4, 2 * hr, chans), BF),
            V((nz, loc, plane), BF),
            V((nz - 1, loc, plane), BF),
        ] + sems,
        compiler_params=pltpu.CompilerParams(
            collective_id=0, has_side_effects=True, vmem_limit_bytes=58 * 1024 * 1024
        ),
    )(
        frames.reshape(loc, plane), conv_weight, time_weight, twt,
        cotangent.reshape(loc, plane),
    )
    return (
        outs[0].reshape(frames.shape), outs[1].reshape(frames.shape), outs[2], outs[3],
    )


def solution(mesh):
    placed = (P("tp", "seq", None), P(None, "tp", None), P(None, "tp", None), P("tp", "seq", None))
    return jax.shard_map(
        per_device,
        mesh=mesh,
        in_specs=placed,
        out_specs=(
            P("tp", "seq", None),
            P("tp", "seq", None),
            P(None, "tp", None),
            P(None, "tp", None),
        ),
        check_vma=False,
    )
```

```python
import functools

import jax
import jax.numpy as jnp
from jax import lax
from jax.experimental import pallas as pl
from jax.experimental.pallas import tpu as pltpu
from jax.sharding import PartitionSpec as P

HGT = 32
WID = 32
BF = jnp.bfloat16
F32 = jnp.float32


def moved(x, down, right):
    if down == 0 and right == 0:
        return x
    plane = x.shape[-1]
    step = (-(WID * down + right)) % plane
    out = pltpu.roll(x, step, 1)
    where = lax.broadcasted_iota(jnp.int32, (1, plane), 1)
    row = where // WID + down
    col = where % WID + right
    ok = (row >= 0) & (row < HGT) & (col >= 0) & (col < WID)
    return jnp.where(ok, out, 0.0)


def nt(a, b):
    return lax.dot_general(a, b, (((1,), (1,)), ((), ())), preferred_element_type=F32)


def tn(a, b):
    return lax.dot_general(a, b, (((0,), (0,)), ((), ())), preferred_element_type=F32)


def nn(a, b):
    return jnp.dot(a, b, preferred_element_type=F32)


def kernel(
    ns, nz, q,
    fr, cw, tw, cot,
    out, fgrad, cgrad, tgrad,
    ffull, cfull, afull, twt, twr, chalo, prod, pre, qrecv, ysend, yrecv,
    shifted, g, gsib, halfb, xin, full, fgsend, fgrecv,
    s_f, r_f, s_c, r_c, s_t, r_t, s_a, r_a, s_g, r_g,
    s_h, r_h, s_q, r_q, s_y, r_y, s_core, r_core, s_x, r_x, s_ag, r_ag, s_fw, r_fw, s_u, r_u,
):
    me = lax.axis_index("seq")
    z = lax.axis_index("tp")
    core = lax.rem(me, 2)
    chip = me // 2
    nc = ns // 2
    hr = nc * q
    loc = fr.shape[0]
    chans = nz * loc

    def zpeer(d):
        return {"tp": lax.rem(z + d, nz)}

    def speer(d):
        return {"seq": lax.rem(me + d + ns, ns)}

    def cpeer(d):
        return {"seq": lax.rem(chip + d, nc) * 2 + core}

    sib = {"seq": chip * 2 + (1 - core)}

    def remote(src, dst, ssem, rsem, dev):
        return pltpu.make_async_remote_copy(
            src_ref=src, dst_ref=dst, send_sem=ssem, recv_sem=rsem,
            device_id=dev, device_id_type=pl.DeviceIdType.MESH,
        )

    barrier = pltpu.get_barrier_semaphore()
    for d in range(1, nz):
        pl.semaphore_signal(barrier, inc=1, device_id=zpeer(d), device_id_type=pl.DeviceIdType.MESH)
    for d in range(1, ns):
        pl.semaphore_signal(barrier, inc=1, device_id=speer(d), device_id_type=pl.DeviceIdType.MESH)
    pl.semaphore_wait(barrier, nz - 1 + ns - 1)

    everything = []

    def go(copies):
        for c in copies:
            c.start()
        everything.extend(copies)
        return copies

    def arrived(copies):
        for c in copies:
            c.wait_recv()

    order = [1, nz - 1] + list(range(2, nz - 1))
    lh = loc // 2
    hops = nz - 1

    def line_copy(buf, ssem, rsem, way, h):
        shard = z - h if way == 0 else z + h
        return remote(
            buf.at[shard], buf.at[shard], ssem.at[way, h], rsem.at[way, h],
            {"tp": z + 1 if way == 0 else z - 1},
        )

    def can_send(way, h):
        if way == 0:
            return (z - h >= 0) & (z + 1 < nz)
        return (z + h < nz) & (z - 1 >= 0)

    def line_send(line, h):
        for way in range(2):
            @pl.when(can_send(way, h))
            def _():
                line_copy(*line, way, h).start()

    def line_recv(line, h):
        buf, ssem, rsem = line
        for way in range(2):
            shard = z - 1 - h if way == 0 else z + 1 + h

            @pl.when(shard >= 0 if way == 0 else shard < nz)
            def _():
                remote(
                    buf.at[shard], buf.at[shard], ssem.at[way, h], rsem.at[way, h],
                    {"tp": z - 1 if way == 0 else z + 1},
                ).wait_recv()

    def line_step(line, h):
        line_recv(line, h)
        if h + 1 < hops:
            line_send(line, h + 1)

    def line_end(line):
        for h in range(hops):
            for way in range(2):
                @pl.when(can_send(way, h))
                def _():
                    line_copy(*line, way, h).wait_send()

    lf, lc, la = (ffull, s_f, r_f), (cfull, s_c, r_c), (afull, s_a, r_a)
    ffull[z] = fr[...]
    line_send(lf, 0)
    cfull[z] = cot[...]
    ch = go([
        remote(cot, chalo.at[0], s_h.at[0], r_h.at[0], speer(1)),
        remote(cot, chalo.at[1], s_h.at[1], r_h.at[1], speer(-1)),
    ])
    rows = pl.ds(pl.multiple_of(core * lh, 16), lh)
    for i in range(nz):
        for k in range(3):
            twt[i, k] = tw[k, :, i * loc:(i + 1) * loc]
    ct = go([
        remote(
            twt.at[lax.rem(z + d, nz), :, rows], twr.at[z, :, rows],
            s_t.at[d], r_t.at[d], zpeer(d),
        )
        for d in order
    ])
    twr[z] = twt[z]
    if 2 * hr > 3 * loc:
        for k in range(4):
            g[k, pl.ds(3 * loc, 2 * hr - 3 * loc), :] = jnp.zeros(
                (2 * hr - 3 * loc, chans), F32
            )
    line_step(lf, 0)
    line_send(lc, 0)
    for h in range(1, hops):
        line_step(lf, h)
        line_step(lc, h - 1)
    cu = []
    for k, d in enumerate(order):
        ct[k].wait_recv()
        part = twr.at[lax.rem(z + nz - d, nz), :, rows]
        cu += go([remote(part, part, s_u.at[d], r_u.at[d], sib)])

    @pl.loop(0, 9)
    def _(t):
        prod[t] = nn(cw[t], ffull[...].reshape(chans, -1))

    total = prod[4]
    for t in range(9):
        if t != 4:
            total = total + moved(prod[t], t // 3 - 1, t % 3 - 1)
    pre[...] = total
    afull[z] = (total / (1.0 + jnp.exp(-total))).astype(BF)
    line_send(la, 0)
    line_step(lc, hops - 1)
    arrived(cu)

    def back_of(k):
        acc = tn(twr[0, k], cfull[0])
        for i in range(1, nz):
            acc = acc + tn(twr[i, k], cfull[i])
        return acc

    prod[5] = back_of(0)
    prod[6] = back_of(2)
    cq = go([
        remote(prod.at[5], qrecv.at[0], s_q.at[0], r_q.at[0], speer(-1)),
        remote(prod.at[6], qrecv.at[1], s_q.at[1], r_q.at[1], speer(1)),
    ])
    prod[8] = back_of(1)
    line_step(la, 0)
    arrived(cq)
    back = prod[8]
    back = back + jnp.where(me < ns - 1, qrecv[0], 0.0)
    back = back + jnp.where(me > 0, qrecv[1], 0.0)
    pr = pre[...]
    sg = 1.0 / (1.0 + jnp.exp(-pr))
    pg = (back * sg * (1.0 + pr * (1.0 - sg))).astype(BF).astype(F32)
    for t in range(9):
        shifted[t] = moved(pg, 1 - t // 3, 1 - t % 3).astype(BF)

    if hops > 1:
        line_step(la, 1)
    prod[0:nz] = tn(cw[0], shifted[0]).reshape(nz, loc, -1)

    @pl.loop(1, 9)
    def _(t):
        prod[0:nz] += tn(cw[t], shifted[t]).reshape(nz, loc, -1)

    for i in range(nz):
        fgsend[i] = prod[i].astype(BF)
    cg = go([
        remote(fgsend.at[lax.rem(z + d, nz)], fgrecv.at[d - 1], s_g.at[d], r_g.at[d], zpeer(d))
        for d in order
    ])

    other = pl.ds(pl.multiple_of((1 - core) * hr, 16), hr)
    mine = pl.ds(pl.multiple_of(core * hr, 16), hr)

    def core_send(k):
        return go([
            remote(g.at[k, other], gsib.at[k], s_core.at[k], r_core.at[k], sib)
        ])

    def chip_send(k):
        gsib[k] = g[k, mine, :] + gsib[k]
        halfb[k] = gsib[k].astype(BF)
        return go([
            remote(
                halfb.at[k, pl.ds(pl.multiple_of(lax.rem(chip + d, nc) * q, 16), q)],
                xin.at[k, d - 1], s_x.at[k, d - 1], r_x.at[k, d - 1], cpeer(d),
            )
            for d in range(1, nc)
        ])

    def chip_sum(k):
        acc = gsib[k, pl.ds(pl.multiple_of(chip * q, 16), q), :]
        for d in range(1, nc):
            acc = acc + xin[k, d - 1].astype(F32)
        own = pl.ds(pl.multiple_of(core * hr + chip * q, 16), q)
        full[k, own, :] = acc.astype(BF)
        return go([
            remote(
                full.at[k, own], full.at[k, own],
                s_ag.at[k, d - 1], r_ag.at[k, d - 1], cpeer(d),
            )
            for d in range(1, nc)
        ])

    def forward(k):
        return go([
            remote(full.at[k, mine], full.at[k, mine], s_fw.at[k], r_fw.at[k], sib)
        ])

    ccore, cx, cag, cfw = {}, {}, {}, {}
    for u in range(3):
        @pl.loop(0, 3)
        def _(v):
            g[u, pl.ds(pl.multiple_of(v * loc, 16), loc), :] = nt(
                shifted[3 * u + v], ffull[...].reshape(chans, -1)
            )
        ccore[u] = core_send(u)
        if u > 0:
            arrived(ccore[u - 1])
            cx[u - 1] = chip_send(u - 1)

    for h in range(2, hops):
        line_step(la, h)
    arrived(ch)

    def time_part(k, rows):
        g[3, pl.ds(k * loc, loc), :] = nt(rows, afull[...].reshape(chans, -1))

    time_part(0, jnp.where(me < ns - 1, chalo[1], jnp.zeros_like(chalo[1])))
    time_part(1, cot[...])
    time_part(2, jnp.where(me > 0, chalo[0], jnp.zeros_like(chalo[0])))
    ccore[3] = core_send(3)
    arrived(ccore[2])
    cx[2] = chip_send(2)

    ysend[0] = nn(tw[0], afull[...].reshape(chans, -1)).astype(BF)
    ysend[1] = nn(tw[2], afull[...].reshape(chans, -1)).astype(BF)
    cy = go([
        remote(ysend.at[0], yrecv.at[0], s_y.at[0], r_y.at[0], speer(1)),
        remote(ysend.at[1], yrecv.at[1], s_y.at[1], r_y.at[1], speer(-1)),
    ])
    arrived(ccore[3])
    cx[3] = chip_send(3)

    for k in range(4):
        arrived(cx[k])
        cag[k] = chip_sum(k)

    mix = nn(tw[1], afull[...].reshape(chans, -1))
    arrived(cy)
    mix = mix + jnp.where(me > 0, yrecv[0].astype(F32), 0.0)
    mix = mix + jnp.where(me < ns - 1, yrecv[1].astype(F32), 0.0)
    out[...] = (fr[...].astype(F32) + mix).astype(BF)

    for k in range(4):
        arrived(cag[k])
        cfw[k] = forward(k)

    arrived(cg)
    acc = cot[...].astype(F32) + prod[z]
    for d in range(nz - 1):
        acc = acc + fgrecv[d].astype(F32)
    fgrad[...] = acc.astype(BF)

    for k in range(4):
        arrived(cfw[k])
        for v in range(3):
            piece = full[k, v * loc:(v + 1) * loc, :]
            if k < 3:
                cgrad[3 * k + v] = piece
            else:
                tgrad[v] = piece
    for c in everything:
        c.wait_send()
    for line in (lf, lc, la):
        line_end(line)


def per_device(frames, conv_weight, time_weight, cotangent):
    loc, _, plane = frames.shape
    ns, nz = lax.axis_size("seq"), lax.axis_size("tp")
    chans = conv_weight.shape[2]
    q = 16 * (-(-3 * loc // (16 * ns)))
    nc = ns // 2
    hr = nc * q
    dma = pltpu.SemaphoreType.DMA
    V = pltpu.VMEM
    sems = [dma((2, nz))] * 4 + [dma((nz,))] * 2 + [dma((2, nz))] * 2 + [dma((nz,))] * 2 + [dma((2,))] * 6 + [dma((4,))] * 2
    sems += [dma((4, nc - 1))] * 4 + [dma((4,))] * 2 + [dma((nz,))] * 2
    outs = pl.pallas_call(
        functools.partial(kernel, ns, nz, q),
        out_shape=(
            jax.ShapeDtypeStruct((loc, plane), BF),
            jax.ShapeDtypeStruct((loc, plane), BF),
            jax.ShapeDtypeStruct((9, loc, chans), BF),
            jax.ShapeDtypeStruct((3, loc, chans), BF),
        ),
        in_specs=[pl.BlockSpec(memory_space=pltpu.VMEM)] * 4,
        out_specs=(pl.BlockSpec(memory_space=pltpu.VMEM),) * 4,
        scratch_shapes=[
            V((nz, loc, plane), BF),
            V((nz, loc, plane), BF),
            V((nz, loc, plane), BF),
            V((nz, 3, loc, loc), BF),
            V((nz, 3, loc, loc), BF),
            V((2, loc, plane), BF),
            V((9, loc, plane), F32),
            V((loc, plane), F32),
            V((2, loc, plane), F32),
            V((2, loc, plane), BF),
            V((2, loc, plane), BF),
            V((9, loc, plane), BF),
            V((4, 2 * hr, chans), F32),
            V((4, hr, chans), F32),
            V((4, hr, chans), BF),
            V((4, nc - 1, q, chans), BF),
            V((4, 2 * hr, chans), BF),
            V((nz, loc, plane), BF),
            V((nz - 1, loc, plane), BF),
        ] + sems,
        compiler_params=pltpu.CompilerParams(
            collective_id=0, has_side_effects=True, vmem_limit_bytes=58 * 1024 * 1024
        ),
    )(
        frames.reshape(loc, plane), conv_weight, time_weight,
        cotangent.reshape(loc, plane),
    )
    return (
        outs[0].reshape(frames.shape), outs[1].reshape(frames.shape),
        outs[2].astype(F32) / ns, outs[3].astype(F32) / ns,
    )


def solution(mesh):
    placed = (P("tp", "seq", None), P(None, "tp", None), P(None, "tp", None), P("tp", "seq", None))
    return jax.shard_map(
        per_device,
        mesh=mesh,
        in_specs=placed,
        out_specs=(
            P("tp", "seq", None),
            P("tp", "seq", None),
            P(None, "tp", None),
            P(None, "tp", None),
        ),
        check_vma=False,
    )
```

```python
import functools

import jax
import jax.numpy as jnp
from jax import lax
from jax.experimental import pallas as pl
from jax.experimental.pallas import tpu as pltpu
from jax.sharding import PartitionSpec as P

HGT = 32
WID = 32
BF = jnp.bfloat16
F32 = jnp.float32


def moved(x, down, right):
    if down == 0 and right == 0:
        return x
    plane = x.shape[-1]
    step = (-(WID * down + right)) % plane
    out = pltpu.roll(x, step, 1)
    where = lax.broadcasted_iota(jnp.int32, (1, plane), 1)
    row = where // WID + down
    col = where % WID + right
    ok = (row >= 0) & (row < HGT) & (col >= 0) & (col < WID)
    return jnp.where(ok, out, 0.0)


def nt(a, b):
    return lax.dot_general(a, b, (((1,), (1,)), ((), ())), preferred_element_type=F32)


def tn(a, b):
    return lax.dot_general(a, b, (((0,), (0,)), ((), ())), preferred_element_type=F32)


def nn(a, b):
    return jnp.dot(a, b, preferred_element_type=F32)


def kernel(
    ns, nz, q,
    fr, cw, tw, cot,
    out, fgrad, cgrad, tgrad,
    ffull, cfull, afull, twt, twr, chalo, prod, pre, qrecv, ysend, yrecv,
    shifted, g, gsib, halfb, xin, full, fgsend, fgrecv,
    s_f, r_f, s_c, r_c, s_t, r_t, s_a, r_a, s_g, r_g,
    s_h, r_h, s_q, r_q, s_y, r_y, s_core, r_core, s_x, r_x, s_ag, r_ag, s_fw, r_fw, s_u, r_u,
):
    me = lax.axis_index("seq")
    z = lax.axis_index("tp")
    core = lax.rem(me, 2)
    chip = me // 2
    nc = ns // 2
    hr = nc * q
    loc = fr.shape[0]
    chans = nz * loc

    def zpeer(d):
        return {"tp": lax.rem(z + d, nz)}

    def speer(d):
        return {"seq": lax.rem(me + d + ns, ns)}

    def cpeer(d):
        return {"seq": lax.rem(chip + d, nc) * 2 + core}

    sib = {"seq": chip * 2 + (1 - core)}

    def remote(src, dst, ssem, rsem, dev):
        return pltpu.make_async_remote_copy(
            src_ref=src, dst_ref=dst, send_sem=ssem, recv_sem=rsem,
            device_id=dev, device_id_type=pl.DeviceIdType.MESH,
        )

    barrier = pltpu.get_barrier_semaphore()
    for d in range(1, nz):
        pl.semaphore_signal(barrier, inc=1, device_id=zpeer(d), device_id_type=pl.DeviceIdType.MESH)
    for d in range(1, ns):
        pl.semaphore_signal(barrier, inc=1, device_id=speer(d), device_id_type=pl.DeviceIdType.MESH)
    pl.semaphore_wait(barrier, nz - 1 + ns - 1)

    everything = []

    def go(copies):
        for c in copies:
            c.start()
        everything.extend(copies)
        return copies

    def arrived(copies):
        for c in copies:
            c.wait_recv()

    order = [1, nz - 1] + list(range(2, nz - 1))
    lh = loc // 2
    hops = nz - 1

    def line_copy(buf, ssem, rsem, way, h):
        shard = z - h if way == 0 else z + h
        return remote(
            buf.at[shard], buf.at[shard], ssem.at[way, h], rsem.at[way, h],
            {"tp": z + 1 if way == 0 else z - 1},
        )

    def can_send(way, h):
        if way == 0:
            return (z - h >= 0) & (z + 1 < nz)
        return (z + h < nz) & (z - 1 >= 0)

    def line_send(line, h):
        for way in range(2):
            @pl.when(can_send(way, h))
            def _():
                line_copy(*line, way, h).start()

    def line_recv(line, h):
        buf, ssem, rsem = line
        for way in range(2):
            shard = z - 1 - h if way == 0 else z + 1 + h

            @pl.when(shard >= 0 if way == 0 else shard < nz)
            def _():
                remote(
                    buf.at[shard], buf.at[shard], ssem.at[way, h], rsem.at[way, h],
                    {"tp": z - 1 if way == 0 else z + 1},
                ).wait_recv()

    def line_step(line, h):
        line_recv(line, h)
        if h + 1 < hops:
            line_send(line, h + 1)

    def line_end(line):
        for h in range(hops):
            for way in range(2):
                @pl.when(can_send(way, h))
                def _():
                    line_copy(*line, way, h).wait_send()

    lf, lc, la = (ffull, s_f, r_f), (cfull, s_c, r_c), (afull, s_a, r_a)
    ffull[z] = fr[...]
    line_send(lf, 0)
    cfull[z] = cot[...]
    ch = go([
        remote(cot, chalo.at[0], s_h.at[0], r_h.at[0], speer(1)),
        remote(cot, chalo.at[1], s_h.at[1], r_h.at[1], speer(-1)),
    ])
    rows = pl.ds(pl.multiple_of(core * lh, 16), lh)
    for i in range(nz):
        for k in range(3):
            twt[i, k] = tw[k, :, i * loc:(i + 1) * loc]
    ct = go([
        remote(
            twt.at[lax.rem(z + d, nz), :, rows], twr.at[z, :, rows],
            s_t.at[d], r_t.at[d], zpeer(d),
        )
        for d in order
    ])
    twr[z] = twt[z]
    if 2 * hr > 3 * loc:
        for k in range(4):
            g[k, pl.ds(3 * loc, 2 * hr - 3 * loc), :] = jnp.zeros(
                (2 * hr - 3 * loc, chans), F32
            )
    line_step(lf, 0)
    line_send(lc, 0)
    for h in range(1, hops):
        line_step(lf, h)
        line_step(lc, h - 1)
    cu = []
    for k, d in enumerate(order):
        ct[k].wait_recv()
        part = twr.at[lax.rem(z + nz - d, nz), :, rows]
        cu += go([remote(part, part, s_u.at[d], r_u.at[d], sib)])

    @pl.loop(0, 9)
    def _(t):
        prod[t] = nn(cw[t], ffull[...].reshape(chans, -1))

    total = prod[4]
    for t in range(9):
        if t != 4:
            total = total + moved(prod[t], t // 3 - 1, t % 3 - 1)
    pre[...] = total
    afull[z] = (total / (1.0 + jnp.exp(-total))).astype(BF)
    line_send(la, 0)
    line_step(lc, hops - 1)
    arrived(cu)

    def back_of(k):
        acc = tn(twr[0, k], cfull[0])
        for i in range(1, nz):
            acc = acc + tn(twr[i, k], cfull[i])
        return acc

    prod[5] = back_of(0)
    prod[6] = back_of(2)
    cq = go([
        remote(prod.at[5], qrecv.at[0], s_q.at[0], r_q.at[0], speer(-1)),
        remote(prod.at[6], qrecv.at[1], s_q.at[1], r_q.at[1], speer(1)),
    ])
    prod[8] = back_of(1)
    line_step(la, 0)
    arrived(cq)
    back = prod[8]
    back = back + jnp.where(me < ns - 1, qrecv[0], 0.0)
    back = back + jnp.where(me > 0, qrecv[1], 0.0)
    pr = pre[...]
    sg = 1.0 / (1.0 + jnp.exp(-pr))
    pg = (back * sg * (1.0 + pr * (1.0 - sg))).astype(BF).astype(F32)
    for t in range(9):
        shifted[t] = moved(pg, 1 - t // 3, 1 - t % 3).astype(BF)

    prod[0:nz] = tn(cw[0], shifted[0]).reshape(nz, loc, -1)

    @pl.loop(1, 9)
    def _(t):
        prod[0:nz] += tn(cw[t], shifted[t]).reshape(nz, loc, -1)

    if hops > 1:
        line_step(la, 1)
    for i in range(nz):
        fgsend[i] = prod[i].astype(BF)
    cg = go([
        remote(fgsend.at[lax.rem(z + d, nz)], fgrecv.at[d - 1], s_g.at[d], r_g.at[d], zpeer(d))
        for d in order
    ])

    other = pl.ds(pl.multiple_of((1 - core) * hr, 16), hr)
    mine = pl.ds(pl.multiple_of(core * hr, 16), hr)

    def core_send(k):
        return go([
            remote(g.at[k, other], gsib.at[k], s_core.at[k], r_core.at[k], sib)
        ])

    def chip_send(k):
        gsib[k] = g[k, mine, :] + gsib[k]
        halfb[k] = gsib[k].astype(BF)
        return go([
            remote(
                halfb.at[k, pl.ds(pl.multiple_of(lax.rem(chip + d, nc) * q, 16), q)],
                xin.at[k, d - 1], s_x.at[k, d - 1], r_x.at[k, d - 1], cpeer(d),
            )
            for d in range(1, nc)
        ])

    def chip_sum(k):
        acc = gsib[k, pl.ds(pl.multiple_of(chip * q, 16), q), :]
        for d in range(1, nc):
            acc = acc + xin[k, d - 1].astype(F32)
        own = pl.ds(pl.multiple_of(core * hr + chip * q, 16), q)
        full[k, own, :] = acc.astype(BF)
        return go([
            remote(
                full.at[k, own], full.at[k, own],
                s_ag.at[k, d - 1], r_ag.at[k, d - 1], cpeer(d),
            )
            for d in range(1, nc)
        ])

    def forward(k):
        return go([
            remote(full.at[k, mine], full.at[k, mine], s_fw.at[k], r_fw.at[k], sib)
        ])

    ccore, cx, cag, cfw = {}, {}, {}, {}
    for u in range(3):
        @pl.loop(0, 3)
        def _(v):
            g[u, pl.ds(pl.multiple_of(v * loc, 16), loc), :] = nt(
                shifted[3 * u + v], ffull[...].reshape(chans, -1)
            )
        ccore[u] = core_send(u)
        if u > 0:
            arrived(ccore[u - 1])
            cx[u - 1] = chip_send(u - 1)

    arrived(ccore[2])
    cx[2] = chip_send(2)
    for k in range(2):
        arrived(cx[k])
        cag[k] = chip_sum(k)
    for h in range(2, hops):
        line_step(la, h)
    arrived(ch)

    def time_part(k, rows):
        g[3, pl.ds(k * loc, loc), :] = nt(rows, afull[...].reshape(chans, -1))

    time_part(0, jnp.where(me < ns - 1, chalo[1], jnp.zeros_like(chalo[1])))
    time_part(1, cot[...])
    time_part(2, jnp.where(me > 0, chalo[0], jnp.zeros_like(chalo[0])))
    ccore[3] = core_send(3)

    ysend[0] = nn(tw[0], afull[...].reshape(chans, -1)).astype(BF)
    ysend[1] = nn(tw[2], afull[...].reshape(chans, -1)).astype(BF)
    cy = go([
        remote(ysend.at[0], yrecv.at[0], s_y.at[0], r_y.at[0], speer(1)),
        remote(ysend.at[1], yrecv.at[1], s_y.at[1], r_y.at[1], speer(-1)),
    ])
    arrived(ccore[3])
    cx[3] = chip_send(3)

    for k in range(2, 4):
        arrived(cx[k])
        cag[k] = chip_sum(k)

    mix = nn(tw[1], afull[...].reshape(chans, -1))
    arrived(cy)
    mix = mix + jnp.where(me > 0, yrecv[0].astype(F32), 0.0)
    mix = mix + jnp.where(me < ns - 1, yrecv[1].astype(F32), 0.0)
    out[...] = (fr[...].astype(F32) + mix).astype(BF)

    for k in range(4):
        arrived(cag[k])
        cfw[k] = forward(k)

    arrived(cg)
    acc = cot[...].astype(F32) + prod[z]
    for d in range(nz - 1):
        acc = acc + fgrecv[d].astype(F32)
    fgrad[...] = acc.astype(BF)

    for k in range(4):
        arrived(cfw[k])
        for v in range(3):
            piece = full[k, v * loc:(v + 1) * loc, :]
            if k < 3:
                cgrad[3 * k + v] = piece
            else:
                tgrad[v] = piece
    for c in everything:
        c.wait_send()
    for line in (lf, lc, la):
        line_end(line)


def per_device(frames, conv_weight, time_weight, cotangent):
    loc, _, plane = frames.shape
    ns, nz = lax.axis_size("seq"), lax.axis_size("tp")
    chans = conv_weight.shape[2]
    q = 16 * (-(-3 * loc // (16 * ns)))
    nc = ns // 2
    hr = nc * q
    dma = pltpu.SemaphoreType.DMA
    V = pltpu.VMEM
    sems = [dma((2, nz))] * 4 + [dma((nz,))] * 2 + [dma((2, nz))] * 2 + [dma((nz,))] * 2 + [dma((2,))] * 6 + [dma((4,))] * 2
    sems += [dma((4, nc - 1))] * 4 + [dma((4,))] * 2 + [dma((nz,))] * 2
    outs = pl.pallas_call(
        functools.partial(kernel, ns, nz, q),
        out_shape=(
            jax.ShapeDtypeStruct((loc, plane), BF),
            jax.ShapeDtypeStruct((loc, plane), BF),
            jax.ShapeDtypeStruct((9, loc, chans), BF),
            jax.ShapeDtypeStruct((3, loc, chans), BF),
        ),
        in_specs=[pl.BlockSpec(memory_space=pltpu.VMEM)] * 4,
        out_specs=(pl.BlockSpec(memory_space=pltpu.VMEM),) * 4,
        scratch_shapes=[
            V((nz, loc, plane), BF),
            V((nz, loc, plane), BF),
            V((nz, loc, plane), BF),
            V((nz, 3, loc, loc), BF),
            V((nz, 3, loc, loc), BF),
            V((2, loc, plane), BF),
            V((9, loc, plane), F32),
            V((loc, plane), F32),
            V((2, loc, plane), F32),
            V((2, loc, plane), BF),
            V((2, loc, plane), BF),
            V((9, loc, plane), BF),
            V((4, 2 * hr, chans), F32),
            V((4, hr, chans), F32),
            V((4, hr, chans), BF),
            V((4, nc - 1, q, chans), BF),
            V((4, 2 * hr, chans), BF),
            V((nz, loc, plane), BF),
            V((nz - 1, loc, plane), BF),
        ] + sems,
        compiler_params=pltpu.CompilerParams(
            collective_id=0, has_side_effects=True, vmem_limit_bytes=58 * 1024 * 1024
        ),
    )(
        frames.reshape(loc, plane), conv_weight, time_weight,
        cotangent.reshape(loc, plane),
    )
    return (
        outs[0].reshape(frames.shape), outs[1].reshape(frames.shape),
        outs[2].astype(F32) / ns, outs[3].astype(F32) / ns,
    )


def solution(mesh):
    placed = (P("tp", "seq", None), P(None, "tp", None), P(None, "tp", None), P("tp", "seq", None))
    return jax.shard_map(
        per_device,
        mesh=mesh,
        in_specs=placed,
        out_specs=(
            P("tp", "seq", None),
            P("tp", "seq", None),
            P(None, "tp", None),
            P(None, "tp", None),
        ),
        check_vma=False,
    )
```
